32 devices in a mesh: groups: 2 (over x), seq: 16 (over z, y, core).
Axes of the slice: x: 2, y: 2, z: 4, core: 2. Of those that a mesh axis runs over, the one named last changes fastest.
Arguments:
- queries: bfloat16 [8192, 2048], P(('groups', 'seq')), parts along dimension 0, may hold values from -6 to 6
- keys: bfloat16 [8192, 2048], P(('groups', 'seq')), parts along dimension 0, may hold values from -6 to 6
- values: bfloat16 [8192, 2048], P(('groups', 'seq')), parts along dimension 0, may hold values from -6 to 6
- gain: float32 [2048], replicated, may hold values from 0.1 to 1.9
Outputs:
- attended: bfloat16 [8192, 2048], P(('groups', 'seq')), parts along dimension 0
The draws below stay inside these ranges and needn't reach their ends.
There are 2 independent parts, one for each index of `groups`. The reference program is written for one: setup_inputs(seed, part) draws one part's arguments, and reference() takes and returns one part's arrays. A program takes and returns all parts, laid end to end along the dimension named above; an argument that names none is the same for every part. Nothing has to cross between parts.
All inputs are finite; a program needn't handle non-finite values.
Results may differ from the reference program's by a relative error of at most 0.01.
Values may be sent and summed in bfloat16 or wider, within the bound.
A program may use at most 192 MiB of HBM per device.

```python
import jax
import jax.numpy as jnp
from jax import lax

HEADS = 32
HEAD_DIM = 64
D = 2048
TOK_DEV = 256
SEQ = 4096
N_SEQ = 16


def block_levels(key, shape, shards, smallest, largest):
    level = 1.0
    for dim, parts in shards:
        draws = jax.random.uniform(jax.random.fold_in(jax.random.fold_in(key, 6), dim), (parts,), jnp.float32, smallest / len(shards), largest / len(shards))
        level = level * jnp.repeat(jnp.exp(draws), shape[dim] // parts).reshape((-1,) + (1,) * (len(shape) - 1 - dim))
    return level


def gaussian(rng, extent, width, bound, shards=(), held_as=jnp.bfloat16):
    result = width * jax.random.normal(rng, extent, jnp.float32)
    if shards:
        result = result * block_levels(rng, extent, shards, -0.22, 0.18)
    return jnp.clip(result, -bound, bound).astype(held_as)


def setup_inputs(seed: int = 0, part: int = 0) -> dict:
    key_list = jax.random.split(jax.random.key(seed), 5)
    own_keys = jax.random.split(jax.random.fold_in(key_list[4], part), 5)
    queries = gaussian(own_keys[0], (SEQ, D), 1.0, 6.0, ((0, 16),))
    keys = gaussian(own_keys[1], (SEQ, D), 1.0, 6.0, ((0, 16),))
    values = gaussian(own_keys[2], (SEQ, D), 1.0, 6.0, ((0, 16),))
    gain = jnp.clip(1.0 + 0.18 * jax.random.normal(key_list[3], (D,), jnp.float32), 0.1, 1.9)
    return {"queries": queries, "keys": keys, "values": values, "gain": gain}


def block_out(fq, fk, vals, prior):
    prior_b = prior.astype(jnp.bfloat16).astype(jnp.float32)
    fq32 = fq.astype(jnp.float32)
    fk32 = fk.astype(jnp.float32)
    v32 = vals.astype(jnp.float32)
    count = fq.shape[0]
    scores = jnp.einsum('thd,shd->hts', fq32, fk32)
    rows = jnp.arange(count)[:, None]
    cols = jnp.arange(count)[None, :]
    scores = jnp.where(cols <= rows, scores, 0.0).astype(jnp.bfloat16).astype(jnp.float32)
    intra = jnp.einsum('hts,she->the', scores, v32)
    inter = jnp.einsum('thd,hde->the', fq32, prior_b)
    return inter + intra

def reference(queries, keys, values, gain):
    blocks = N_SEQ
    fq = jax.nn.relu(queries).reshape(blocks, TOK_DEV, HEADS, HEAD_DIM)
    fk = jax.nn.relu(keys).reshape(blocks, TOK_DEV, HEADS, HEAD_DIM)
    vals = values.reshape(blocks, TOK_DEV, HEADS, HEAD_DIM)

    def step(prior, item):
        q_blk, k_blk, v_blk = item
        numer = block_out(q_blk, k_blk, v_blk, prior)
        state = jnp.einsum('thd,the->hde', k_blk.astype(jnp.float32), v_blk.astype(jnp.float32))
        return (prior + state, numer)
    init = jnp.zeros((HEADS, HEAD_DIM, HEAD_DIM), jnp.float32)
    final, numer = lax.scan(step, init, (fq, fk, vals))
    mean_sq = lax.optimization_barrier(jnp.mean(numer * numer, axis=-1, keepdims=True))
    normed = numer * lax.rsqrt(mean_sq + 1e-05)
    normed = normed.reshape(blocks * TOK_DEV, HEADS * HEAD_DIM) * gain[None, :]
    return normed.astype(jnp.bfloat16)
```

```python
import functools

import jax
import jax.numpy as jnp
from jax import lax
from jax.experimental import pallas as pl
from jax.experimental.pallas import tpu as pltpu
from jax.sharding import PartitionSpec as P

HEAD_DIM = 64
PAIR = 128
GRP = 256
BF = jnp.bfloat16
F32 = jnp.float32


def kernel(n, q_hbm, k_hbm, v_hbm, gain_ref, out_hbm,
           q, k, v, o, numer, st, s0, r0, cs, r1, pf, r2, s3, r3, own,
           in_sem, out_sem, c_send, c_recv, a_send, a_recv, b_send, b_recv):
    count, width = q.shape
    chips = n // 2
    half = width // 2
    per_half = half // GRP
    rows = st.shape[1] // chips
    me = lax.axis_index("seq")
    core = lax.rem(me, 2)
    chip = me // 2
    other = 1 - core
    partner = me + 1 - 2 * core

    def load(src, dst, h, sem):
        at = pl.ds(pl.multiple_of(h * half, half), half)
        return pltpu.make_async_copy(src.at[:, at], dst.at[:, at], in_sem.at[sem])

    loads = [load(k_hbm, k, other, 0), load(v_hbm, v, other, 1),
             load(k_hbm, k, core, 2), load(v_hbm, v, core, 3),
             pltpu.make_async_copy(q_hbm, q, in_sem.at[4])]
    for c in loads:
        c.start()

    barrier = pltpu.get_barrier_semaphore()
    pl.semaphore_signal(barrier, inc=1, device_id={"seq": partner},
                        device_id_type=pl.DeviceIdType.MESH)

    def greet(d, _):
        to = lax.rem(chip + d, chips) * 2 + core
        pl.semaphore_signal(barrier, inc=1, device_id={"seq": to},
                            device_id_type=pl.DeviceIdType.MESH)
        return 0

    lax.fori_loop(1, chips, greet, 0)

    lane = lax.broadcasted_iota(jnp.int32, (HEAD_DIM, PAIR), 1)
    first = lane < HEAD_DIM

    def state_group(h, g):
        at = pl.ds(pl.multiple_of(h * half + g * GRP, GRP), GRP)
        fk = jnp.maximum(k[:, at], 0)
        m = lax.dot_general(fk, v[:, at], (((0,), (0,)), ((), ())),
                            preferred_element_type=F32)
        for p in range(GRP // PAIR):
            a = p * PAIR
            blk = jnp.where(first, m[a:a + HEAD_DIM, a:a + PAIR],
                            m[a + HEAD_DIM:a + PAIR, a:a + PAIR])
            row = pl.multiple_of((g * 2 + p) * HEAD_DIM, HEAD_DIM)
            st[h, pl.ds(row, HEAD_DIM), :] = blk

    def state_half(h):
        def body(g, _):
            state_group(h, g)
            return 0
        lax.fori_loop(0, per_half, body, 0)

    loads[0].wait()
    loads[1].wait()
    state_half(other)
    s0[...] = st[other].astype(BF)

    pl.semaphore_wait(barrier, chips)

    def core_copy(src, dst, i):
        return pltpu.make_async_remote_copy(
            src_ref=src, dst_ref=dst, send_sem=c_send.at[i], recv_sem=c_recv.at[i],
            device_id={"seq": partner}, device_id_type=pl.DeviceIdType.MESH)

    x0 = core_copy(s0, r0, 0)
    x0.start()
    loads[2].wait()
    loads[3].wait()
    state_half(core)
    x0.wait_recv()
    cs[...] = (st[core] + r0[...].astype(F32)).astype(BF).reshape(cs.shape)

    def scatter(src, dst, ssem, rsem, to, slot):
        return pltpu.make_async_remote_copy(
            src_ref=src.at[to], dst_ref=dst.at[slot],
            send_sem=ssem.at[to], recv_sem=rsem.at[slot],
            device_id={"seq": to * 2 + core}, device_id_type=pl.DeviceIdType.MESH)

    def start_all(src, dst, ssem, rsem):
        def body(d, _):
            scatter(src, dst, ssem, rsem, lax.rem(chip + d, chips), chip).start()
            return 0
        lax.fori_loop(1, chips, body, 0)
        dst[chip] = src[chip]

    def recv_all(src, dst, ssem, rsem):
        def body(d, _):
            frm = lax.rem(chip + d, chips)
            scatter(src, dst, ssem, rsem, frm, frm).wait_recv()
            return 0
        lax.fori_loop(1, chips, body, 0)

    def sent_all(src, dst, ssem, rsem):
        def body(d, _):
            scatter(src, dst, ssem, rsem, lax.rem(chip + d, chips), chip).wait_send()
            return 0
        lax.fori_loop(1, chips, body, 0)

    head = lax.broadcasted_iota(jnp.int32, (count, GRP), 1) // HEAD_DIM
    causal = (lax.broadcasted_iota(jnp.int32, (count, count), 1)
              <= lax.broadcasted_iota(jnp.int32, (count, count), 0))

    def intra(g, _):
        at = pl.ds(pl.multiple_of(g * GRP, GRP), GRP)
        fq = jnp.maximum(q[:, at], 0)
        fk = jnp.maximum(k[:, at], 0)
        vv = v[:, at]
        zero = jnp.zeros_like(fq)
        acc = None
        for i in range(GRP // HEAD_DIM):
            s = lax.dot_general(jnp.where(head == i, fq, zero), fk, (((1,), (1,)), ((), ())),
                                preferred_element_type=F32)
            s = jnp.where(causal, s, 0.0).astype(BF)
            part = jnp.dot(s, jnp.where(head == i, vv, zero), preferred_element_type=F32)
            acc = part if acc is None else acc + part
        numer[:, at] = acc
        return 0

    start_all(cs, r1, a_send, a_recv)
    loads[4].wait()
    lax.fori_loop(0, per_half, intra, 0)
    recv_all(cs, r1, a_send, a_recv)

    def hop(i, acc):
        pf[i] = acc.astype(BF)
        return acc + r1[i].astype(F32)

    lax.fori_loop(0, chips, hop, jnp.zeros((rows, PAIR), F32))
    start_all(pf, r2, b_send, b_recv)
    lax.fori_loop(per_half, 2 * per_half, intra, 0)
    recv_all(pf, r2, b_send, b_recv)

    before = r2[...].reshape(own.shape).astype(F32)
    s3[...] = (before + jnp.where(core == 0, st[core], 0.0)).astype(BF)
    x3 = core_copy(s3, r3, 1)
    x3.start()
    own[...] = (before + jnp.where(core == 0, 0.0, r0[...].astype(F32))).astype(BF)

    square = (lax.broadcasted_iota(jnp.int32, (GRP, GRP), 0) // HEAD_DIM
              == lax.broadcasted_iota(jnp.int32, (GRP, GRP), 1) // HEAD_DIM)
    ones = jnp.where(square, 1.0 / HEAD_DIM, 0.0).astype(BF)

    def finish(h, prior):
        def body(g, _):
            at = pl.ds(pl.multiple_of(h * half + g * GRP, GRP), GRP)
            fq = jnp.maximum(q[:, at], 0)
            pair = [prior[pl.ds(pl.multiple_of((g * 2 + p) * HEAD_DIM, HEAD_DIM), HEAD_DIM), :]
                    for p in range(GRP // PAIR)]
            wide = jnp.concatenate(pair, axis=1)
            full = jnp.concatenate([wide] * (GRP // HEAD_DIM), axis=0)
            full = jnp.where(square, full, jnp.zeros_like(full))
            num = numer[:, at] + jnp.dot(fq, full, preferred_element_type=F32)
            mean = jnp.dot((num * num).astype(BF), ones, preferred_element_type=F32)
            o[:, at] = (num * lax.rsqrt(mean + 1e-05) * gain_ref[:, at]).astype(BF)
            return 0
        lax.fori_loop(0, per_half, body, 0)
        at = pl.ds(pl.multiple_of(h * half, half), half)
        return pltpu.make_async_copy(o.at[:, at], out_hbm.at[:, at], out_sem.at[h])

    w0 = finish(core, own)
    w0.start()
    x3.wait_recv()
    w1 = finish(other, r3)
    w1.start()
    x0.wait_send()
    x3.wait_send()
    sent_all(cs, r1, a_send, a_recv)
    sent_all(pf, r2, b_send, b_recv)
    w0.wait()
    w1.wait()


def on_device(n, queries, keys, values, gain):
    count, width = queries.shape
    chips = n // 2
    half_rows = width // 2 // PAIR * HEAD_DIM
    piece = half_rows // chips
    any_spec = pl.BlockSpec(memory_space=pl.ANY)
    vmem = pltpu.VMEM
    dma = pltpu.SemaphoreType.DMA
    return pl.pallas_call(
        functools.partial(kernel, n),
        out_shape=jax.ShapeDtypeStruct((count, width), BF),
        in_specs=[any_spec, any_spec, any_spec, pl.BlockSpec(memory_space=pltpu.VMEM)],
        out_specs=any_spec,
        scratch_shapes=[
            vmem((count, width), BF), vmem((count, width), BF), vmem((count, width), BF),
            vmem((count, width), BF), vmem((count, width), F32),
            vmem((2, half_rows, PAIR), F32),
            vmem((half_rows, PAIR), BF), vmem((half_rows, PAIR), BF),
            vmem((chips, piece, PAIR), BF), vmem((chips, piece, PAIR), BF),
            vmem((chips, piece, PAIR), BF), vmem((chips, piece, PAIR), BF),
            vmem((half_rows, PAIR), BF), vmem((half_rows, PAIR), BF), vmem((half_rows, PAIR), BF),
            dma((5,)), dma((2,)), dma((2,)), dma((2,)),
            dma((chips,)), dma((chips,)), dma((chips,)), dma((chips,)),
        ],
        compiler_params=pltpu.CompilerParams(
            collective_id=0, has_side_effects=True, vmem_limit_bytes=40 * 1024 * 1024),
    )(queries, keys, values, gain.reshape(1, width))


def solution(mesh):
    n = mesh.shape["seq"]
    rows = P(("groups", "seq"), None)
    return jax.shard_map(
        functools.partial(on_device, n), mesh=mesh,
        in_specs=(rows, rows, rows, P()), out_specs=rows, check_vma=False)
```

```python
import functools

import jax
import jax.numpy as jnp
from jax import lax
from jax.experimental import pallas as pl
from jax.experimental.pallas import tpu as pltpu
from jax.sharding import PartitionSpec as P

HEAD_DIM = 64
PAIR = 128
GRP = 256
BF = jnp.bfloat16
F32 = jnp.float32


def kernel(n, q_hbm, k_hbm, v_hbm, gain_ref, o,
           q, k, v, numer, st, s0, r0, cs, r1, pf, r2, s3, r3, own,
           in_sem, c_send, c_recv, a_send, a_recv, b_send, b_recv):
    count, width = q.shape
    chips = n // 2
    half = width // 2
    per_half = half // GRP
    rows = st.shape[1] // chips
    me = lax.axis_index("seq")
    core = lax.rem(me, 2)
    chip = me // 2
    other = 1 - core
    partner = me + 1 - 2 * core

    def load(src, dst, h, sem):
        at = pl.ds(pl.multiple_of(h * half, half), half)
        return pltpu.make_async_copy(src.at[:, at], dst.at[:, at], in_sem.at[sem])

    loads = [load(k_hbm, k, other, 0), load(v_hbm, v, other, 1),
             load(k_hbm, k, core, 2), load(v_hbm, v, core, 3),
             pltpu.make_async_copy(q_hbm, q, in_sem.at[4])]
    for c in loads:
        c.start()

    barrier = pltpu.get_barrier_semaphore()
    pl.semaphore_signal(barrier, inc=1, device_id={"seq": partner},
                        device_id_type=pl.DeviceIdType.MESH)

    def greet(d, _):
        to = lax.rem(chip + d, chips) * 2 + core
        pl.semaphore_signal(barrier, inc=1, device_id={"seq": to},
                            device_id_type=pl.DeviceIdType.MESH)
        return 0

    lax.fori_loop(1, chips, greet, 0)

    lane = lax.broadcasted_iota(jnp.int32, (HEAD_DIM, PAIR), 1)
    first = lane < HEAD_DIM

    def state_group(h, g):
        at = pl.ds(pl.multiple_of(h * half + g * GRP, GRP), GRP)
        fk = jnp.maximum(k[:, at], 0)
        m = lax.dot_general(fk, v[:, at], (((0,), (0,)), ((), ())),
                            preferred_element_type=F32)
        for p in range(GRP // PAIR):
            a = p * PAIR
            blk = jnp.where(first, m[a:a + HEAD_DIM, a:a + PAIR],
                            m[a + HEAD_DIM:a + PAIR, a:a + PAIR])
            row = pl.multiple_of((g * 2 + p) * HEAD_DIM, HEAD_DIM)
            st[h, pl.ds(row, HEAD_DIM), :] = blk

    def state_half(h):
        def body(g, _):
            state_group(h, g)
            return 0
        lax.fori_loop(0, per_half, body, 0)

    loads[0].wait()
    loads[1].wait()
    state_half(other)
    s0[...] = st[other].astype(BF)

    pl.semaphore_wait(barrier, chips)

    def core_copy(src, dst, i):
        return pltpu.make_async_remote_copy(
            src_ref=src, dst_ref=dst, send_sem=c_send.at[i], recv_sem=c_recv.at[i],
            device_id={"seq": partner}, device_id_type=pl.DeviceIdType.MESH)

    x0 = core_copy(s0, r0, 0)
    x0.start()
    loads[2].wait()
    loads[3].wait()
    state_half(core)
    x0.wait_recv()
    cs[...] = (st[core] + r0[...].astype(F32)).astype(BF).reshape(cs.shape)

    def scatter(src, dst, ssem, rsem, to, slot):
        return pltpu.make_async_remote_copy(
            src_ref=src.at[to], dst_ref=dst.at[slot],
            send_sem=ssem.at[to], recv_sem=rsem.at[slot],
            device_id={"seq": to * 2 + core}, device_id_type=pl.DeviceIdType.MESH)

    def start_all(src, dst, ssem, rsem):
        def body(d, _):
            scatter(src, dst, ssem, rsem, lax.rem(chip + d, chips), chip).start()
            return 0
        lax.fori_loop(1, chips, body, 0)
        dst[chip] = src[chip]

    def recv_all(src, dst, ssem, rsem):
        def body(d, _):
            frm = lax.rem(chip + d, chips)
            scatter(src, dst, ssem, rsem, frm, frm).wait_recv()
            return 0
        lax.fori_loop(1, chips, body, 0)

    def sent_all(src, dst, ssem, rsem):
        def body(d, _):
            scatter(src, dst, ssem, rsem, lax.rem(chip + d, chips), chip).wait_send()
            return 0
        lax.fori_loop(1, chips, body, 0)

    head = lax.broadcasted_iota(jnp.int32, (count, GRP), 1) // HEAD_DIM
    causal = (lax.broadcasted_iota(jnp.int32, (count, count), 1)
              <= lax.broadcasted_iota(jnp.int32, (count, count), 0))

    def intra(g, _):
        at = pl.ds(pl.multiple_of(g * GRP, GRP), GRP)
        fq = jnp.maximum(q[:, at], 0)
        fk = jnp.maximum(k[:, at], 0)
        vv = v[:, at]
        zero = jnp.zeros_like(fq)
        acc = None
        for i in range(GRP // HEAD_DIM):
            s = lax.dot_general(jnp.where(head == i, fq, zero), fk, (((1,), (1,)), ((), ())),
                                preferred_element_type=F32)
            s = jnp.where(causal, s, 0.0).astype(BF)
            part = jnp.dot(s, jnp.where(head == i, vv, zero), preferred_element_type=F32)
            acc = part if acc is None else acc + part
        numer[:, at] = acc
        return 0

    start_all(cs, r1, a_send, a_recv)
    loads[4].wait()
    lax.fori_loop(0, per_half, intra, 0)
    recv_all(cs, r1, a_send, a_recv)

    def hop(i, acc):
        pf[i] = acc.astype(BF)
        return acc + r1[i].astype(F32)

    lax.fori_loop(0, chips, hop, jnp.zeros((rows, PAIR), F32))
    start_all(pf, r2, b_send, b_recv)
    lax.fori_loop(per_half, 2 * per_half, intra, 0)
    recv_all(pf, r2, b_send, b_recv)

    before = r2[...].reshape(own.shape).astype(F32)
    s3[...] = (before + jnp.where(core == 0, st[core], 0.0)).astype(BF)
    x3 = core_copy(s3, r3, 1)
    x3.start()
    own[...] = (before + jnp.where(core == 0, 0.0, r0[...].astype(F32))).astype(BF)

    square = (lax.broadcasted_iota(jnp.int32, (GRP, GRP), 0) // HEAD_DIM
              == lax.broadcasted_iota(jnp.int32, (GRP, GRP), 1) // HEAD_DIM)
    ones = jnp.where(square, 1.0 / HEAD_DIM, 0.0).astype(BF)

    def finish(h, prior):
        def body(g, _):
            at = pl.ds(pl.multiple_of(h * half + g * GRP, GRP), GRP)
            fq = jnp.maximum(q[:, at], 0)
            pair = [prior[pl.ds(pl.multiple_of((g * 2 + p) * HEAD_DIM, HEAD_DIM), HEAD_DIM), :]
                    for p in range(GRP // PAIR)]
            wide = jnp.concatenate(pair, axis=1)
            full = jnp.concatenate([wide] * (GRP // HEAD_DIM), axis=0)
            full = jnp.where(square, full, jnp.zeros_like(full))
            num = numer[:, at] + jnp.dot(fq, full, preferred_element_type=F32)
            mean = jnp.dot((num * num).astype(BF), ones, preferred_element_type=F32)
            o[:, at] = (num * lax.rsqrt(mean + 1e-05) * gain_ref[:, at]).astype(BF)
            return 0
        lax.fori_loop(0, per_half, body, 0)

    finish(core, own)
    x3.wait_recv()
    finish(other, r3)
    x0.wait_send()
    x3.wait_send()
    sent_all(cs, r1, a_send, a_recv)
    sent_all(pf, r2, b_send, b_recv)


def on_device(n, queries, keys, values, gain):
    count, width = queries.shape
    chips = n // 2
    half_rows = width // 2 // PAIR * HEAD_DIM
    piece = half_rows // chips
    hbm = pl.BlockSpec(memory_space=pltpu.HBM)
    vmem = pltpu.VMEM
    dma = pltpu.SemaphoreType.DMA
    return pl.pallas_call(
        functools.partial(kernel, n),
        out_shape=jax.ShapeDtypeStruct((count, width), BF),
        in_specs=[hbm, hbm, hbm, pl.BlockSpec(memory_space=pltpu.VMEM)],
        out_specs=pl.BlockSpec(memory_space=pltpu.VMEM),
        scratch_shapes=[
            vmem((count, width), BF), vmem((count, width), BF), vmem((count, width), BF),
            vmem((count, width), F32),
            vmem((2, half_rows, PAIR), F32),
            vmem((half_rows, PAIR), BF), vmem((half_rows, PAIR), BF),
            vmem((chips, piece, PAIR), BF), vmem((chips, piece, PAIR), BF),
            vmem((chips, piece, PAIR), BF), vmem((chips, piece, PAIR), BF),
            vmem((half_rows, PAIR), BF), vmem((half_rows, PAIR), BF), vmem((half_rows, PAIR), BF),
            dma((5,)), dma((2,)), dma((2,)),
            dma((chips,)), dma((chips,)), dma((chips,)), dma((chips,)),
        ],
        compiler_params=pltpu.CompilerParams(
            collective_id=0, has_side_effects=True, vmem_limit_bytes=62 * 1024 * 1024),
    )(queries, keys, values, gain.reshape(1, width))


def solution(mesh):
    n = mesh.shape["seq"]
    rows = P(("groups", "seq"), None)
    return jax.shard_map(
        functools.partial(on_device, n), mesh=mesh,
        in_specs=(rows, rows, rows, P()), out_specs=rows, check_vma=False)
```

```python
import functools

import jax
import jax.numpy as jnp
from jax import lax
from jax.experimental import pallas as pl
from jax.experimental.pallas import tpu as pltpu
from jax.sharding import PartitionSpec as P

HEAD_DIM = 64
PAIR = 128
GRP = 256
BF = jnp.bfloat16
F32 = jnp.float32


def kernel(n, q_hbm, k_hbm, v_hbm, o,
           q, k, v, numer, st, s0, r0, cf, cy, ry, qs, r1, pf, r2, sy, qown, qother, s3, r3, own,
           in_sem, c_send, c_recv, y_send, y_recv, a_send, a_recv, b_send, b_recv):
    count, width = q.shape
    quads = n // 4
    half = width // 2
    per_half = half // GRP
    rows = qs.shape[1]
    me = lax.axis_index("seq")
    core = lax.rem(me, 2)
    side = lax.rem(me // 2, 2)
    quad = me // 4
    other = 1 - core
    across = 1 - side
    partner = me + 1 - 2 * core
    opposite = me + 2 - 4 * side

    def load(src, dst, h, sem):
        at = pl.ds(pl.multiple_of(h * half, half), half)
        return pltpu.make_async_copy(src.at[:, at], dst.at[:, at], in_sem.at[sem])

    loads = [load(k_hbm, k, other, 0), load(v_hbm, v, other, 1),
             load(k_hbm, k, core, 2), load(v_hbm, v, core, 3),
             pltpu.make_async_copy(q_hbm, q, in_sem.at[4])]
    for c in loads:
        c.start()

    barrier = pltpu.get_barrier_semaphore()
    for to in (partner, opposite):
        pl.semaphore_signal(barrier, inc=1, device_id={"seq": to},
                            device_id_type=pl.DeviceIdType.MESH)

    def greet(d, _):
        to = lax.rem(quad + d, quads) * 4 + side * 2 + core
        pl.semaphore_signal(barrier, inc=1, device_id={"seq": to},
                            device_id_type=pl.DeviceIdType.MESH)
        return 0

    lax.fori_loop(1, quads, greet, 0)

    lane = lax.broadcasted_iota(jnp.int32, (HEAD_DIM, PAIR), 1)
    first = lane < HEAD_DIM

    def state_group(h, g):
        at = pl.ds(pl.multiple_of(h * half + g * GRP, GRP), GRP)
        fk = jnp.maximum(k[:, at], 0)
        m = lax.dot_general(fk, v[:, at], (((0,), (0,)), ((), ())),
                            preferred_element_type=F32)
        for p in range(GRP // PAIR):
            a = p * PAIR
            blk = jnp.where(first, m[a:a + HEAD_DIM, a:a + PAIR],
                            m[a + HEAD_DIM:a + PAIR, a:a + PAIR])
            row = pl.multiple_of((g * 2 + p) * HEAD_DIM, HEAD_DIM)
            st[h, pl.ds(row, HEAD_DIM), :] = blk

    def state_half(h):
        def body(g, _):
            state_group(h, g)
            return 0
        lax.fori_loop(0, per_half, body, 0, unroll=True)

    loads[0].wait()
    loads[1].wait()
    state_half(other)
    s0[...] = st[other].astype(BF)

    pl.semaphore_wait(barrier, quads + 1)

    def swap(src, dst, ssem, rsem, i, to):
        return pltpu.make_async_remote_copy(
            src_ref=src, dst_ref=dst, send_sem=ssem.at[i], recv_sem=rsem.at[i],
            device_id={"seq": to}, device_id_type=pl.DeviceIdType.MESH)

    x0 = swap(s0, r0, c_send, c_recv, 0, partner)
    x0.start()
    loads[2].wait()
    loads[3].wait()
    state_half(core)
    x0.wait_recv()
    cf[...] = (st[core] + r0[...].astype(F32)).reshape(cf.shape)
    cy[...] = cf[across].astype(BF)
    y1 = swap(cy, ry, y_send, y_recv, 0, opposite)
    y1.start()

    def scatter(src, dst, ssem, rsem, to, slot):
        return pltpu.make_async_remote_copy(
            src_ref=src.at[to], dst_ref=dst.at[slot],
            send_sem=ssem.at[to], recv_sem=rsem.at[slot],
            device_id={"seq": to * 4 + side * 2 + core}, device_id_type=pl.DeviceIdType.MESH)

    def start_all(src, dst, ssem, rsem):
        def body(d, _):
            scatter(src, dst, ssem, rsem, lax.rem(quad + d, quads), quad).start()
            return 0
        lax.fori_loop(1, quads, body, 0)
        dst[quad] = src[quad]

    def recv_all(src, dst, ssem, rsem):
        def body(d, _):
            frm = lax.rem(quad + d, quads)
            scatter(src, dst, ssem, rsem, frm, frm).wait_recv()
            return 0
        lax.fori_loop(1, quads, body, 0)

    def sent_all(src, dst, ssem, rsem):
        def body(d, _):
            scatter(src, dst, ssem, rsem, lax.rem(quad + d, quads), quad).wait_send()
            return 0
        lax.fori_loop(1, quads, body, 0)

    head = lax.broadcasted_iota(jnp.int32, (count, GRP), 1) // HEAD_DIM
    causal = (lax.broadcasted_iota(jnp.int32, (count, count), 1)
              <= lax.broadcasted_iota(jnp.int32, (count, count), 0))

    def intra(g, _):
        at = pl.ds(pl.multiple_of(g * GRP, GRP), GRP)
        fq = jnp.maximum(q[:, at], 0)
        fk = jnp.maximum(k[:, at], 0)
        vv = v[:, at]
        zero = jnp.zeros_like(fq)
        acc = None
        for i in range(GRP // HEAD_DIM):
            s = lax.dot_general(jnp.where(head == i, fq, zero), fk, (((1,), (1,)), ((), ())),
                                preferred_element_type=F32)
            s = jnp.where(causal, s, 0.0).astype(BF)
            part = jnp.dot(s, jnp.where(head == i, vv, zero), preferred_element_type=F32)
            acc = part if acc is None else acc + part
        numer[:, at] = acc
        return 0

    def work(a, b):
        lax.fori_loop(a * per_half // 2, b * per_half // 2, intra, 0, unroll=True)

    loads[4].wait()
    work(0, 1)
    y1.wait_recv()
    qs[...] = (cf[side] + ry[...].astype(F32)).astype(BF).reshape(qs.shape)
    start_all(qs, r1, a_send, a_recv)
    work(1, 2)
    recv_all(qs, r1, a_send, a_recv)

    def hop(i, acc):
        pf[i] = acc.astype(BF)
        return acc + r1[i].astype(F32)

    lax.fori_loop(0, quads, hop, jnp.zeros((rows, PAIR), F32), unroll=True)
    start_all(pf, r2, b_send, b_recv)
    work(2, 3)
    recv_all(pf, r2, b_send, b_recv)
    earlier = r2[...].reshape(sy.shape).astype(F32)
    sy[...] = (earlier + jnp.where(side == 0, cf[side], 0.0)).astype(BF)
    y2 = swap(sy, qother, y_send, y_recv, 1, opposite)
    y2.start()
    qown[...] = earlier + jnp.where(side == 0, 0.0, ry[...].astype(F32))
    work(3, 4)
    y2.wait_recv()
    got = qother[...].astype(F32)
    mine = qown[...]
    before = jnp.concatenate([jnp.where(side == 0, mine, got),
                              jnp.where(side == 0, got, mine)], axis=0)

    s3[...] = (before + jnp.where(core == 0, st[core], 0.0)).astype(BF)
    x3 = swap(s3, r3, c_send, c_recv, 1, partner)
    x3.start()
    own[...] = (before + jnp.where(core == 0, 0.0, r0[...].astype(F32))).astype(BF)

    square = (lax.broadcasted_iota(jnp.int32, (GRP, GRP), 0) // HEAD_DIM
              == lax.broadcasted_iota(jnp.int32, (GRP, GRP), 1) // HEAD_DIM)
    ones = jnp.where(square, 1.0 / HEAD_DIM, 0.0).astype(BF)

    def finish(h, prior):
        def body(g, _):
            at = pl.ds(pl.multiple_of(h * half + g * GRP, GRP), GRP)
            fq = jnp.maximum(q[:, at], 0)
            pair = [prior[pl.ds(pl.multiple_of((g * 2 + p) * HEAD_DIM, HEAD_DIM), HEAD_DIM), :]
                    for p in range(GRP // PAIR)]
            wide = jnp.concatenate(pair, axis=1)
            full = jnp.concatenate([wide] * (GRP // HEAD_DIM), axis=0)
            full = jnp.where(square, full, jnp.zeros_like(full))
            num = numer[:, at] + jnp.dot(fq, full, preferred_element_type=F32)
            mean = jnp.dot((num * num).astype(BF), ones, preferred_element_type=F32)
            o[:, at] = (num * lax.rsqrt(mean + 1e-05)).astype(BF)
            return 0
        lax.fori_loop(0, per_half, body, 0, unroll=True)

    finish(core, own)
    x3.wait_recv()
    finish(other, r3)
    x0.wait_send()
    x3.wait_send()
    y1.wait_send()
    y2.wait_send()
    sent_all(qs, r1, a_send, a_recv)
    sent_all(pf, r2, b_send, b_recv)


def on_device(n, queries, keys, values, gain):
    count, width = queries.shape
    quads = n // 4
    half_rows = width // 2 // PAIR * HEAD_DIM
    quarter = half_rows // 2
    piece = quarter // quads
    hbm = pl.BlockSpec(memory_space=pltpu.HBM)
    vmem = pltpu.VMEM
    dma = pltpu.SemaphoreType.DMA
    normed = pl.pallas_call(
        functools.partial(kernel, n),
        out_shape=jax.ShapeDtypeStruct((count, width), BF),
        in_specs=[hbm] * 3,
        out_specs=pl.BlockSpec(memory_space=pltpu.VMEM),
        scratch_shapes=[
            vmem((count, width), BF), vmem((count, width), BF), vmem((count, width), BF),
            vmem((count, width), F32),
            vmem((2, half_rows, PAIR), F32),
            vmem((half_rows, PAIR), BF), vmem((half_rows, PAIR), BF),
            vmem((2, quarter, PAIR), F32), vmem((quarter, PAIR), BF), vmem((quarter, PAIR), BF),
            vmem((quads, piece, PAIR), BF), vmem((quads, piece, PAIR), BF),
            vmem((quads, piece, PAIR), BF), vmem((quads, piece, PAIR), BF),
            vmem((quarter, PAIR), BF), vmem((quarter, PAIR), F32), vmem((quarter, PAIR), BF),
            vmem((half_rows, PAIR), BF), vmem((half_rows, PAIR), BF), vmem((half_rows, PAIR), BF),
            dma((5,)), dma((2,)), dma((2,)), dma((2,)), dma((2,)),
            dma((quads,)), dma((quads,)), dma((quads,)), dma((quads,)),
        ],
        compiler_params=pltpu.CompilerParams(
            collective_id=0, has_side_effects=True, vmem_limit_bytes=52 * 1024 * 1024),
    )(queries, keys, values)
    return (normed.astype(F32) * gain[None, :]).astype(BF)


def solution(mesh):
    n = mesh.shape["seq"]
    rows = P(("groups", "seq"), None)
    return jax.shard_map(
        functools.partial(on_device, n), mesh=mesh,
        in_specs=(rows, rows, rows, P()), out_specs=rows, check_vma=False)
```

```python
import functools

import jax
import jax.numpy as jnp
from jax import lax
from jax.experimental import pallas as pl
from jax.experimental.pallas import tpu as pltpu
from jax.sharding import PartitionSpec as P

HEAD_DIM = 64
PAIR = 128
GRP = 256
BF = jnp.bfloat16
F32 = jnp.float32


def kernel(n, q_hbm, k_hbm, v_hbm, o,
           q, k, v, numer, st, s0, r0, cs, r1, pf, r2, s3, r3, own,
           in_sem, c_send, c_recv, a_send, a_recv, b_send, b_recv):
    count, width = q.shape
    chips = n // 2
    half = width // 2
    per_half = half // GRP
    rows = st.shape[1] // chips
    me = lax.axis_index("seq")
    core = lax.rem(me, 2)
    chip = me // 2
    other = 1 - core
    partner = me + 1 - 2 * core

    def load(src, dst, h, sem):
        at = pl.ds(pl.multiple_of(h * half, half), half)
        return pltpu.make_async_copy(src.at[:, at], dst.at[:, at], in_sem.at[sem])

    loads = [load(k_hbm, k, other, 0), load(v_hbm, v, other, 1),
             load(k_hbm, k, core, 2), load(v_hbm, v, core, 3),
             pltpu.make_async_copy(q_hbm, q, in_sem.at[4])]
    for c in loads:
        c.start()

    barrier = pltpu.get_barrier_semaphore()
    pl.semaphore_signal(barrier, inc=1, device_id={"seq": partner},
                        device_id_type=pl.DeviceIdType.MESH)

    def greet(d, _):
        to = lax.rem(chip + d, chips) * 2 + core
        pl.semaphore_signal(barrier, inc=1, device_id={"seq": to},
                            device_id_type=pl.DeviceIdType.MESH)
        return 0

    lax.fori_loop(1, chips, greet, 0)

    lane = lax.broadcasted_iota(jnp.int32, (HEAD_DIM, PAIR), 1)
    first = lane < HEAD_DIM

    def state_group(h, g):
        at = pl.ds(pl.multiple_of(h * half + g * GRP, GRP), GRP)
        fk = jnp.maximum(k[:, at], 0)
        m = lax.dot_general(fk, v[:, at], (((0,), (0,)), ((), ())),
                            preferred_element_type=F32)
        for p in range(GRP // PAIR):
            a = p * PAIR
            blk = jnp.where(first, m[a:a + HEAD_DIM, a:a + PAIR],
                            m[a + HEAD_DIM:a + PAIR, a:a + PAIR])
            row = pl.multiple_of((g * 2 + p) * HEAD_DIM, HEAD_DIM)
            st[h, pl.ds(row, HEAD_DIM), :] = blk

    def state_half(h):
        def body(g, _):
            state_group(h, g)
            return 0
        lax.fori_loop(0, per_half, body, 0, unroll=True)

    loads[0].wait()
    loads[1].wait()
    state_half(other)
    s0[...] = st[other].astype(BF)

    pl.semaphore_wait(barrier, chips)

    def core_copy(src, dst, i):
        return pltpu.make_async_remote_copy(
            src_ref=src, dst_ref=dst, send_sem=c_send.at[i], recv_sem=c_recv.at[i],
            device_id={"seq": partner}, device_id_type=pl.DeviceIdType.MESH)

    x0 = core_copy(s0, r0, 0)
    x0.start()
    loads[2].wait()
    loads[3].wait()
    state_half(core)
    x0.wait_recv()
    cs[...] = (st[core] + r0[...].astype(F32)).astype(BF).reshape(cs.shape)

    def scatter(src, dst, ssem, rsem, to, slot):
        return pltpu.make_async_remote_copy(
            src_ref=src.at[to], dst_ref=dst.at[slot],
            send_sem=ssem.at[to], recv_sem=rsem.at[slot],
            device_id={"seq": to * 2 + core}, device_id_type=pl.DeviceIdType.MESH)

    def start_all(src, dst, ssem, rsem):
        def body(d, _):
            scatter(src, dst, ssem, rsem, lax.rem(chip + d, chips), chip).start()
            return 0
        lax.fori_loop(1, chips, body, 0)
        dst[chip] = src[chip]

    def recv_all(src, dst, ssem, rsem):
        def body(d, _):
            frm = lax.rem(chip + d, chips)
            scatter(src, dst, ssem, rsem, frm, frm).wait_recv()
            return 0
        lax.fori_loop(1, chips, body, 0)

    def sent_all(src, dst, ssem, rsem):
        def body(d, _):
            scatter(src, dst, ssem, rsem, lax.rem(chip + d, chips), chip).wait_send()
            return 0
        lax.fori_loop(1, chips, body, 0)

    head = lax.broadcasted_iota(jnp.int32, (count, GRP), 1) // HEAD_DIM
    causal = (lax.broadcasted_iota(jnp.int32, (count, count), 1)
              <= lax.broadcasted_iota(jnp.int32, (count, count), 0))

    def intra(g, _):
        at = pl.ds(pl.multiple_of(g * GRP, GRP), GRP)
        fq = jnp.maximum(q[:, at], 0)
        fk = jnp.maximum(k[:, at], 0)
        vv = v[:, at]
        zero = jnp.zeros_like(fq)
        acc = None
        for i in range(GRP // HEAD_DIM):
            s = lax.dot_general(jnp.where(head == i, fq, zero), fk, (((1,), (1,)), ((), ())),
                                preferred_element_type=F32)
            s = jnp.where(causal, s, 0.0).astype(BF)
            part = jnp.dot(s, jnp.where(head == i, vv, zero), preferred_element_type=F32)
            acc = part if acc is None else acc + part
        numer[:, at] = acc
        return 0

    start_all(cs, r1, a_send, a_recv)
    loads[4].wait()
    lax.fori_loop(0, per_half, intra, 0, unroll=True)
    recv_all(cs, r1, a_send, a_recv)

    def hop(i, acc):
        pf[i] = acc.astype(BF)
        return acc + r1[i].astype(F32)

    lax.fori_loop(0, chips, hop, jnp.zeros((rows, PAIR), F32))
    start_all(pf, r2, b_send, b_recv)
    lax.fori_loop(per_half, 2 * per_half, intra, 0, unroll=True)
    recv_all(pf, r2, b_send, b_recv)

    before = r2[...].reshape(own.shape).astype(F32)
    s3[...] = (before + jnp.where(core == 0, st[core], 0.0)).astype(BF)
    x3 = core_copy(s3, r3, 1)
    x3.start()
    own[...] = (before + jnp.where(core == 0, 0.0, r0[...].astype(F32))).astype(BF)

    square = (lax.broadcasted_iota(jnp.int32, (GRP, GRP), 0) // HEAD_DIM
              == lax.broadcasted_iota(jnp.int32, (GRP, GRP), 1) // HEAD_DIM)
    ones = jnp.where(square, 1.0 / HEAD_DIM, 0.0).astype(BF)

    def finish(h, prior):
        def body(g, _):
            at = pl.ds(pl.multiple_of(h * half + g * GRP, GRP), GRP)
            fq = jnp.maximum(q[:, at], 0)
            pair = [prior[pl.ds(pl.multiple_of((g * 2 + p) * HEAD_DIM, HEAD_DIM), HEAD_DIM), :]
                    for p in range(GRP // PAIR)]
            wide = jnp.concatenate(pair, axis=1)
            full = jnp.concatenate([wide] * (GRP // HEAD_DIM), axis=0)
            full = jnp.where(square, full, jnp.zeros_like(full))
            num = numer[:, at] + jnp.dot(fq, full, preferred_element_type=F32)
            mean = jnp.dot((num * num).astype(BF), ones, preferred_element_type=F32)
            o[:, at] = (num * lax.rsqrt(mean + 1e-05)).astype(BF)
            return 0
        lax.fori_loop(0, per_half, body, 0, unroll=True)

    finish(core, own)
    x3.wait_recv()
    finish(other, r3)
    x0.wait_send()
    x3.wait_send()
    sent_all(cs, r1, a_send, a_recv)
    sent_all(pf, r2, b_send, b_recv)


def on_device(n, queries, keys, values, gain):
    count, width = queries.shape
    chips = n // 2
    half_rows = width // 2 // PAIR * HEAD_DIM
    piece = half_rows // chips
    hbm = pl.BlockSpec(memory_space=pltpu.HBM)
    vmem = pltpu.VMEM
    dma = pltpu.SemaphoreType.DMA
    normed = pl.pallas_call(
        functools.partial(kernel, n),
        out_shape=jax.ShapeDtypeStruct((count, width), BF),
        in_specs=[hbm] * 3,
        out_specs=pl.BlockSpec(memory_space=pltpu.VMEM),
        scratch_shapes=[
            vmem((count, width), BF), vmem((count, width), BF), vmem((count, width), BF),
            vmem((count, width), F32),
            vmem((2, half_rows, PAIR), F32),
            vmem((half_rows, PAIR), BF), vmem((half_rows, PAIR), BF),
            vmem((chips, piece, PAIR), BF), vmem((chips, piece, PAIR), BF),
            vmem((chips, piece, PAIR), BF), vmem((chips, piece, PAIR), BF),
            vmem((half_rows, PAIR), BF), vmem((half_rows, PAIR), BF), vmem((half_rows, PAIR), BF),
            dma((5,)), dma((2,)), dma((2,)),
            dma((chips,)), dma((chips,)), dma((chips,)), dma((chips,)),
        ],
        compiler_params=pltpu.CompilerParams(
            collective_id=0, has_side_effects=True, vmem_limit_bytes=52 * 1024 * 1024),
    )(queries, keys, values)
    return (normed.astype(F32) * gain[None, :]).astype(BF)


def solution(mesh):
    n = mesh.shape["seq"]
    rows = P(("groups", "seq"), None)
    return jax.shard_map(
        functools.partial(on_device, n), mesh=mesh,
        in_specs=(rows, rows, rows, P()), out_specs=rows, check_vma=False)
```
